512 devices in a mesh: dp: 64 (over x, y, core), tensor: 8 (over z).
Axes of the slice: x: 4, y: 8, z: 8, core: 2. Of those that a mesh axis runs over, the one named last changes fastest.
Arguments:
- features: bfloat16 [32768, 128], P(('dp', 'tensor')), may hold values from -24 to 24
- output_gradient: bfloat16 [32768, 28672], P('dp', 'tensor'), may hold values from -0.03125 to 0.03125
- live_token_count: int32 [64], replicated, may hold values from 1 to 512, 24576 in all
- former_range_lengths: int32 [64], replicated, may hold values from 1792 to 12544, as said below
- target_range_lengths: int32 [63], replicated, may hold values from 1790 to 12659, as said below
- keeper_rank_list: int32 [63], replicated, may hold values from 0 to 63, as said below
- former_master_weight: float32 [8, 802816], P('tensor', 'dp'), may hold values from -6 to 6
- former_first_moment: float32 [8, 802816], P('tensor', 'dp'), may hold values from -6 to 6
- former_second_moment: float32 [8, 802816], P('tensor', 'dp'), may hold values from 0.05 to 4
Outputs:
- new_master: float32 [8, 810176], P('tensor', 'dp')
- new_first: float32 [8, 810176], P('tensor', 'dp')
- new_second: float32 [8, 810176], P('tensor', 'dp')
The draws below stay inside these ranges and needn't reach their ends.
Inputs may be any that keep to these rules, and one draw needn't show every extreme that they name: `former_range_lengths`: summing to 458752; the boundary after the first k ranges lies within 2688 of k * 7168; the longest range is exactly 12544. `target_range_lengths`: summing to 458752; the boundary after the first k ranges lies between -2688 and 2690 from (k * 458752) // 63; the longest range is exactly 12659. `keeper_rank_list`: Increasing; exactly one data rank is missing.
All inputs are finite; a program needn't handle non-finite values.
Results may differ from the reference program's by a relative error of at most 0.0003.
Values may be sent and summed in bfloat16 or wider, within the bound.
A program may use at most 64 MiB of HBM per device.

```python
import math
import jax
import jax.numpy as jnp
import numpy as np
from jax import lax

FF = 28672
ROWS = 128
TOK_DEV = 512
TOKENS = 32768
FF_SHARD = 3584
PARAMS = 458752
BLOCK = 7168
SPREAD = 2688
OLD_CAP = 12544
NEW_CAP = 12659
N_DP = 64
N_TENSOR = 8


def draw_former_range_lengths(key, part):
    key = jax.random.fold_in(key, 11)
    inner_key, pick_key = jax.random.split(key)
    shifts = jax.random.randint(inner_key, (N_DP - 1,), -SPREAD, SPREAD + 1).astype(jnp.int32)
    chosen = jax.random.randint(pick_key, (), 1, N_DP - 1)
    shifts = shifts.at[chosen - 1].set(-SPREAD).at[chosen].set(SPREAD)
    inner = jnp.arange(1, N_DP, dtype=jnp.int32) * BLOCK + shifts
    bounds = jnp.concatenate([jnp.zeros((1,), jnp.int32), inner, jnp.full((1,), PARAMS, jnp.int32)])
    return (bounds[1:] - bounds[:-1]).astype(jnp.int32)


def draw_target_range_lengths(key, part):
    key = jax.random.fold_in(key, 12)
    inner_key, pick_key = jax.random.split(key)
    bases = jnp.arange(N_DP, dtype=jnp.int32) * PARAMS // (N_DP - 1)
    shifts = jax.random.randint(inner_key, (N_DP - 2,), -SPREAD, SPREAD + 1).astype(jnp.int32)
    chosen = jax.random.randint(pick_key, (), 1, N_DP - 2)
    base_length = bases[chosen + 1] - bases[chosen]
    shifts = shifts.at[chosen - 1].set(-SPREAD).at[chosen].set(NEW_CAP - base_length - SPREAD)
    inner = bases[1:N_DP - 1] + shifts
    bounds = jnp.concatenate([jnp.zeros((1,), jnp.int32), inner, jnp.full((1,), PARAMS, jnp.int32)])
    return (bounds[1:] - bounds[:-1]).astype(jnp.int32)


def draw_keeper_rank_list(key, part):
    key = jax.random.fold_in(key, 13)
    missing = jax.random.randint(key, (), 0, N_DP)
    steps_all = jnp.arange(N_DP - 1, dtype=jnp.int32)
    return (steps_all + (steps_all >= missing).astype(jnp.int32)).astype(jnp.int32)


def raised(result, stream_key, source, target, shards_of, factor):
    owner, partner = [(jnp.arange(result.shape[position]) // (result.shape[position] // shards_of)).reshape([-1 if axis == position else 1 for axis in range(result.ndim)]) for position in (source, target)]
    chosen = jax.random.permutation(stream_key, shards_of)[partner]
    strong = (owner == chosen) | (owner == (partner + shards_of // 2) % shards_of)
    return jnp.where(strong, factor * result, result)


def shard_levels(stream_key, extent, pieces, least, high):
    factor_of, own = 1.0, jax.random.fold_in(stream_key, 6)
    for position, parts in pieces:
        draws = jnp.exp(jax.random.uniform(jax.random.fold_in(own, position), (parts,), jnp.float32, least / len(pieces), high / len(pieces)))
        factor_of = factor_of * jnp.repeat(draws, extent[position] // parts).reshape([-1 if axis == position else 1 for axis in range(len(extent))])
    return factor_of


def split_up(count, total, bound, lean):
    loads = [(1 << 20) // math.isqrt(rank ** lean) + 1 for rank in range(2, count + 1)]
    spare, holding = total - bound - (count - 1), [1] * (count - 1)
    while spare > 0:
        free = [i for i in range(count - 1) if holding[i] < bound]
        pool, budget = sum([loads[i] for i in free]), spare
        for i in free:
            more = min(bound - holding[i], max(1, budget * loads[i] // pool), spare)
            holding[i] = holding[i] + more
            spare = spare - more
    return np.array([bound] + holding)


def ragged_sizes(rng, amount, total, limit, skew):
    if amount == 2:
        one = jax.random.randint(rng, (), max(1, total - limit), min(limit, total - 1) + 1)
        return jnp.stack([one, total - one])
    sizes = jnp.asarray(split_up(amount, total, limit, skew), jnp.int32)
    twos = (amount - 1) // 2
    donor, taker = sizes[1:1 + 2 * twos:2], sizes[2:2 + 2 * twos:2]
    margin = jnp.minimum(donor - 1, limit - taker)
    passed = jax.random.randint(jax.random.fold_in(rng, 1), (twos,), 0, 1 << 20) % (margin + 1)
    sizes = sizes.at[1:1 + 2 * twos:2].set(donor - passed).at[2:2 + 2 * twos:2].set(taker + passed)
    return sizes[jax.random.permutation(jax.random.fold_in(rng, 2), amount)]


def gaussian(rng, extent, scale, bound, cuts=(), kind=jnp.bfloat16):
    values = jax.random.normal(rng, extent, jnp.float32) * scale
    if len(cuts) > 0:
        values = shard_levels(rng, extent, cuts, -0.22, 0.18) * values
    return jnp.clip(values, min=-bound, max=bound).astype(kind)


def noise_with(stream_key, shape, scale, limit, shards, heavy, held_as=jnp.bfloat16):
    array = scale * jax.random.normal(stream_key, shape, jnp.float32)
    if shards:
        array = array * shard_levels(stream_key, shape, shards, -0.22, 0.18)
    return jnp.clip(raised(array, jax.random.fold_in(stream_key, 3), *heavy), -limit, limit).astype(held_as)


def setup_inputs(seed: int = 0) -> dict:
    key_list = jax.random.split(jax.random.key(seed), 10)
    features = noise_with(key_list[0], (TOKENS, ROWS), 1.0, 24.0, ((0, 512),), (0, 1, 128, 5.5))
    output_gradient = gaussian(key_list[1], (TOKENS, FF), TOKENS ** -0.5, 0.03125, ((0, 64), (1, 8)))
    live_token_count = ragged_sizes(key_list[2], N_DP, 3 * TOKENS // 4, TOK_DEV, 1).astype(jnp.int32)
    former_range_lengths = draw_former_range_lengths(jax.random.fold_in(key_list[9], 71), 0)
    target_range_lengths = draw_target_range_lengths(jax.random.fold_in(key_list[9], 71), 0)
    keeper_rank_list = draw_keeper_rank_list(jax.random.fold_in(key_list[9], 71), 0)
    former_master_weight = gaussian(key_list[6], (N_TENSOR, N_DP * OLD_CAP), 1.0, 6.0, ((0, 8), (1, 64)), jnp.float32)
    former_first_moment = gaussian(key_list[7], (N_TENSOR, N_DP * OLD_CAP), 1.0, 6.0, ((0, 8), (1, 64)), jnp.float32)
    former_second_moment = jnp.clip(jnp.exp(math.log(4.0) - 4.3820266 * jax.random.uniform(key_list[8], (N_TENSOR, N_DP * OLD_CAP), jnp.float32) ** shard_levels(key_list[8], (N_TENSOR, N_DP * OLD_CAP), ((0, 8), (1, 64)), -0.2, 0.2)), 0.05, 4.0)
    return dict(features=features, output_gradient=output_gradient, live_token_count=live_token_count, former_range_lengths=former_range_lengths, target_range_lengths=target_range_lengths, keeper_rank_list=keeper_rank_list, former_master_weight=former_master_weight, former_first_moment=former_first_moment, former_second_moment=former_second_moment)


BETA_ONE = 0.9
BETA_TWO = 0.95
EPSILON = 1e-08
DECAY = 0.1
LEARN_RATE = 0.02
CORRECT_ONE = 1.0 - 2.6561398887587544e-05
CORRECT_TWO = 1.0 - 0.005920529220333998

def range_bounds(lengths):
    return jnp.concatenate([jnp.zeros((1,), jnp.int32), jnp.cumsum(lengths).astype(jnp.int32)])

def adamw_step(master, moment_one, moment_two, gradient, in_range):
    first_next = BETA_ONE * moment_one + (1.0 - BETA_ONE) * gradient
    second_next = BETA_TWO * moment_two + (1.0 - BETA_TWO) * gradient * gradient
    update = first_next / CORRECT_ONE / (jnp.sqrt(second_next / CORRECT_TWO) + EPSILON)
    master_next = master - LEARN_RATE * (update + DECAY * master)
    return (jnp.where(in_range, master_next, jnp.zeros_like(master_next)), jnp.where(in_range, first_next, jnp.zeros_like(first_next)), jnp.where(in_range, second_next, jnp.zeros_like(second_next)))

def reference(features, output_gradient, live_token_count, former_range_lengths, target_range_lengths, keeper_rank_list, former_master_weight, former_first_moment, former_second_moment):
    every_rank_list = jnp.arange(N_DP, dtype=jnp.int32)
    owner_flag = jnp.any(keeper_rank_list[None, :] == every_rank_list[:, None], axis=1)
    row_ids = jnp.arange(TOKENS, dtype=jnp.int32)
    row_rank = row_ids // TOK_DEV
    live_rows = (row_ids % TOK_DEV < live_token_count[row_rank]) & owner_flag[row_rank]
    masked = jnp.where(live_rows[:, None], features, jnp.zeros_like(features))
    gradient = jnp.dot(masked.T, output_gradient, preferred_element_type=jnp.float32)
    grad_flat = gradient.reshape(ROWS, N_TENSOR, FF_SHARD).transpose(1, 0, 2).reshape(N_TENSOR, PARAMS)
    old_bounds = range_bounds(former_range_lengths)
    positions = jnp.arange(PARAMS, dtype=jnp.int32)
    holder = (jnp.searchsorted(old_bounds, positions, side='right') - 1).astype(jnp.int32)
    old_slots = (holder * OLD_CAP + positions - old_bounds[holder]).astype(jnp.int32)
    new_bounds = range_bounds(target_range_lengths)
    cursor_position = jnp.minimum(lax.optimization_barrier(jnp.sum((keeper_rank_list[None, :] < every_rank_list[:, None]).astype(jnp.int32), axis=1)), N_DP - 2)
    begins = new_bounds[cursor_position]
    lengths_all = jnp.where(owner_flag, target_range_lengths[cursor_position], 0)
    slot_ids = jnp.arange(NEW_CAP, dtype=jnp.int32)
    in_range = (slot_ids[None, :] < lengths_all[:, None]).reshape(-1)
    targets = jnp.where(in_range, (begins[:, None] + slot_ids[None, :]).reshape(-1), 0).astype(jnp.int32)
    sources = old_slots[targets]
    slot_grad = jnp.where(in_range[None, :], grad_flat[:, targets], jnp.float32(0.0))
    slot_master = jnp.where(in_range[None, :], former_master_weight[:, sources], jnp.float32(0.0))
    slot_first = jnp.where(in_range[None, :], former_first_moment[:, sources], jnp.float32(0.0))
    slot_second = jnp.where(in_range[None, :], former_second_moment[:, sources], jnp.float32(0.0))
    new_master, new_first, new_second = adamw_step(slot_master, slot_first, slot_second, slot_grad, in_range[None, :])
    return (new_master, new_first, new_second)
```

```python
import functools
import jax
import jax.numpy as jnp
from jax import lax
from jax.experimental import pallas as pl
from jax.experimental.pallas import tpu as pltpu
from jax.sharding import PartitionSpec as P

BETA_ONE = 0.9
BETA_TWO = 0.95
EPSILON = 1e-08
DECAY = 0.1
LEARN_RATE = 0.02
CORRECT_ONE = 1.0 - 2.6561398887587544e-05
CORRECT_TWO = 1.0 - 0.005920529220333998

NX, NY, NC = 4, 8, 2
NDP = NX * NY * NC
NZ = 8
ROWS = 128
COLS = 28
TOK = 512
TOK_Z = TOK // NZ
LANES = 128
BLOCK = 7168
OLD_CAP = 12544
OLD_ROWS = OLD_CAP // LANES
NEW_CAP = 12659
OUT_ROWS = 99
WIN = 104
GRAD_ROWS = 304
SLOTS = 20
FRONT = 2
OFFSETS = (-2, -1, 1, 2)

CHUNKS = ((0, 20, "x"), (20, 8, "y"))


def main_kernel(
    live_in, keeper_in, former_in, target_in, feat, og, st0, st1, st2, states, grad, meta,
    og_v, feat_all, mt, live, keeper, former, target, *rest,
):
    n = len(CHUNKS)
    part, core, r1, r2, fin = (rest[k * n : (k + 1) * n] for k in range(5))
    (ag_s, ag_r, og_sem, st_s, st_r, st_loc, co_s, co_r, s1_s, s1_r, s2_s, s2_r, rd_s, rd_r,
     in_sem) = rest[5 * n :]
    me = lax.axis_index("dp")
    z = lax.axis_index("tensor")
    c = lax.rem(me, NC)
    y = lax.rem(me // NC, NY)
    x = me // (NC * NY)

    def dp_of(x_, y_, c_):
        return (x_ * NY + y_) * NC + c_

    def dev(d, z_):
        return {"dp": d, "tensor": z_}

    def at_x(o):
        return dev(dp_of(lax.rem(x + o, NX), y, c), z)

    def at_y(o):
        return dev(dp_of(x, lax.rem(y + o, NY), c), z)

    def at_z(o):
        return dev(me, lax.rem(z + o, NZ))

    def at_d(o):
        return dev(lax.rem(me + o + NDP, NDP), z)

    sibling = dev(dp_of(x, y, 1 - c), z)

    my_rows = pl.ds(pl.multiple_of(z * TOK_Z, TOK_Z), TOK_Z)
    small = []
    for i, (a, b) in enumerate(
        ((keeper_in, keeper), (target_in, target), (former_in, former), (live_in, live),
         (feat, feat_all.at[my_rows]))
    ):
        small.append(pltpu.make_async_copy(a, b, in_sem.at[i]))
        small[-1].start()
    local = []
    for k, (j0, nj, _) in enumerate(CHUNKS):
        cols = pl.ds(j0 * LANES, nj * LANES)
        local.append(pltpu.make_async_copy(og.at[:, cols], og_v.at[:, cols], og_sem.at[k]))
        local[-1].start()
    mine = []
    for a, st in enumerate((st0, st1, st2)):
        mine.append(pltpu.make_async_copy(st, states.at[FRONT + 5 * a + 2], st_loc.at[a]))
        mine[-1].start()

    barrier = pltpu.get_barrier_semaphore()
    peers = (
        [at_z(o) for o in range(1, NZ)]
        + [sibling]
        + [at_x(o) for o in range(1, NX)]
        + [at_y(o) for o in range(1, NY)]
        + [at_d(o) for o in OFFSETS]
    )
    for p in peers:
        pl.semaphore_signal(barrier, inc=1, device_id=p, device_id_type=pl.DeviceIdType.MESH)
    pl.semaphore_wait(barrier, len(peers))

    sent = []

    def send(src, dst, s_sem, r_sem, to):
        copy = pltpu.make_async_remote_copy(
            src_ref=src, dst_ref=dst, send_sem=s_sem, recv_sem=r_sem,
            device_id=to, device_id_type=pl.DeviceIdType.MESH,
        )
        copy.start()
        sent.append(copy)
        return copy

    gather = [
        send(feat, feat_all.at[my_rows], ag_s.at[o - 1], ag_r.at[o - 1], at_z(o))
        for o in (4, 3, 5, 2, 6, 1, 7)
    ]

    moved = []
    for a, st in enumerate((st0, st1, st2)):
        for i, o in enumerate(OFFSETS):
            moved.append(
                send(st, states.at[FRONT + 5 * a + 2 - o], st_s.at[4 * a + i], st_r.at[4 * a + i], at_d(o))
            )

    for copy in small:
        copy.wait()

    def add_up(ref, count, stop):
        return lax.fori_loop(
            0, count, lambda i, t: t + jnp.where(i < stop, ref[i], 0), jnp.int32(0)
        )

    low = jnp.minimum(me, NDP - 2)
    high = jnp.maximum(me - 1, 0)
    at_same = (me < NDP - 1) & (keeper[low] == me)
    at_before = (me > 0) & (keeper[high] == me)
    owner = at_same | at_before
    cursor = jnp.where(at_same, low, high)
    begin = jnp.where(
        at_same, add_up(target, NDP - 1, low), add_up(target, NDP - 1, high)
    )
    meta[0] = begin
    meta[1] = jnp.where(owner, jnp.where(at_same, target[low], target[high]), 0)
    meta[2] = begin - (me - 2) * BLOCK
    edge = add_up(former, NDP, me - 2)
    for i in range(5):
        s = me - 2 + i
        inside = (s >= 0) & (s < NDP)
        size = jnp.where(inside, former[jnp.clip(s, 0, NDP - 1)], 0)
        meta[3 + 2 * i] = edge
        meta[4 + 2 * i] = edge + size
        edge = edge + size
    live_count = jnp.where(owner, live[me], 0)

    for copy in gather:
        copy.wait_recv()

    tok = lax.broadcasted_iota(jnp.int32, (TOK, ROWS), 0)
    masked = jnp.where(tok < live_count, feat_all[...].astype(jnp.float32), 0.0).astype(jnp.bfloat16)
    out_row = lax.broadcasted_iota(jnp.int32, (ROWS, ROWS), 0)
    in_row = lax.broadcasted_iota(jnp.int32, (ROWS, ROWS), 1)
    for w, order in enumerate(("x", "y")):
        cc, b, i = out_row // 64, lax.rem(out_row // 2, 32), lax.rem(out_row, 2)
        if order == "x":
            bx, by = b // NY, lax.rem(b, NY)
        else:
            bx, by = lax.rem(b, NX), b // NX
        pick = (in_row == ((bx * NY + by) * NC + cc) * 2 + i).astype(jnp.float32).astype(jnp.bfloat16)
        mt[w] = lax.dot_general(
            pick, masked, (((1,), (1,)), ((), ())), preferred_element_type=jnp.float32
        ).astype(jnp.bfloat16)

    cores = []
    for k, (j0, nj, order) in enumerate(CHUNKS):
        local[k].wait()
        w = 0 if order == "x" else 1
        for j in range(0, nj, 2):
            out = jnp.dot(
                mt[w],
                og_v[:, (j0 + j) * LANES : (j0 + j + 2) * LANES],
                preferred_element_type=jnp.float32,
            )
            part[k][pl.ds(j, ROWS, stride=nj), :] = out[:, :LANES]
            part[k][pl.ds(j + 1, ROWS, stride=nj), :] = out[:, LANES:]
        half = 64 * nj
        cores.append(
            send(
                part[k].at[pl.ds(pl.multiple_of((1 - c) * half, half), half)],
                core[k], co_s.at[k], co_r.at[k], sibling,
            )
        )

    def plan(order):
        if order == "x":
            return NX, x, at_x, NY, y, at_y
        return NY, y, at_y, NX, x, at_x

    first = []
    for k, (j0, nj, order) in enumerate(CHUNKS):
        n1, i1, at1, n2, i2, at2 = plan(order)
        g1 = 64 * nj // n1
        half = 64 * nj
        cores[k].wait_recv()
        copies = []
        for o in list(range(1, n1)) + [0]:
            row = pl.multiple_of(lax.rem(i1 + o, n1) * g1, g1)
            core[k][pl.ds(row, g1)] = core[k][pl.ds(row, g1)] + part[k][pl.ds(pl.multiple_of(c * half + row, g1), g1)]
            if o:
                copies.append(
                    send(core[k].at[pl.ds(row, g1)], r1[k].at[pl.ds((o - 1) * g1, g1)],
                         s1_s.at[k, o - 1], s1_r.at[k, o - 1], at1(o))
                )
        first.append(copies)

    second = []
    for k, (j0, nj, order) in enumerate(CHUNKS):
        n1, i1, at1, n2, i2, at2 = plan(order)
        g1 = 64 * nj // n1
        g2 = 2 * nj
        for copy in first[k]:
            copy.wait_recv()
        copies = []
        for o in list(range(1, n2)) + [0]:
            row = pl.multiple_of(lax.rem(i2 + o, n2) * g2, g2)
            base = pl.multiple_of(i1 * g1 + row, g2)
            total = core[k][pl.ds(base, g2)]
            for q in range(n1 - 1):
                total = total + r1[k][pl.ds(pl.multiple_of(q * g1 + row, g2), g2)]
            spot = pl.ds(pl.multiple_of(c * 64 * nj + row, g2), g2)
            part[k][spot] = total
            if o:
                copies.append(
                    send(part[k].at[spot], r2[k].at[pl.ds((o - 1) * g2, g2)],
                         s2_s.at[k, o - 1], s2_r.at[k, o - 1], at2(o))
                )
        second.append(copies)

    third = []
    for k, (j0, nj, order) in enumerate(CHUNKS):
        n1, i1, at1, n2, i2, at2 = plan(order)
        g2 = 2 * nj
        for copy in second[k]:
            copy.wait_recv()
        total = part[k][pl.ds(pl.multiple_of(c * 64 * nj + i2 * g2, g2), g2)]
        for q in range(n2 - 1):
            total = total + r2[k][q * g2 : (q + 1) * g2]
        fin[k][2 * g2 : 3 * g2] = total
        third.append([
            send(fin[k].at[pl.ds(2 * g2, g2)], fin[k].at[pl.ds((2 - o) * g2, g2)],
                 rd_s.at[k, i], rd_r.at[k, i], at_d(o))
            for i, o in enumerate(OFFSETS)
        ])

    for k, (j0, nj, order) in enumerate(CHUNKS):
        for copy in third[k]:
            copy.wait_recv()
        for m in range(10):
            grad[m * COLS + j0 : m * COLS + j0 + nj] = fin[k][m * nj : (m + 1) * nj]

    for copy in moved:
        copy.wait_recv()
    for copy in sent:
        copy.wait_send()
    for copy in mine:
        copy.wait()


def gather_and_reduce(features, og, live, former, target, keeper, st0, st1, st2):
    n = len(CHUNKS)
    vmem = lambda rows, dtype=jnp.float32: pltpu.VMEM((rows, LANES), dtype)
    scratch = [
        pltpu.VMEM((TOK, COLS * LANES), jnp.bfloat16),
        vmem(TOK, jnp.bfloat16),
        pltpu.VMEM((2, ROWS, TOK), jnp.bfloat16),
    ] + [pltpu.SMEM(v.shape, jnp.int32) for v in (live, keeper, former, target)]
    counts = [(NX, NY) if order == "x" else (NY, NX) for _, _, order in CHUNKS]
    scratch += [vmem(ROWS * nj) for _, nj, _ in CHUNKS]
    scratch += [vmem(64 * nj) for _, nj, _ in CHUNKS]
    scratch += [vmem((n1 - 1) * 64 * nj // n1) for (_, nj, _), (n1, n2) in zip(CHUNKS, counts)]
    scratch += [vmem((n2 - 1) * 2 * nj) for (_, nj, _), (n1, n2) in zip(CHUNKS, counts)]
    scratch += [vmem(10 * nj) for _, nj, _ in CHUNKS]
    dma = lambda *s: pltpu.SemaphoreType.DMA(s)
    scratch += [
        dma(7), dma(7), dma(n), dma(12), dma(12), dma(3), dma(n), dma(n),
        dma(n, 7), dma(n, 7), dma(n, 7), dma(n, 7), dma(n, 4), dma(n, 4), dma(5),
    ]
    smem = pl.BlockSpec(memory_space=pltpu.SMEM)
    anyw = pl.BlockSpec(memory_space=pl.ANY)
    return pl.pallas_call(
        main_kernel,
        out_shape=(
            jax.ShapeDtypeStruct((SLOTS, 1, OLD_CAP), jnp.float32),
            jax.ShapeDtypeStruct((GRAD_ROWS, LANES), jnp.float32),
            jax.ShapeDtypeStruct((16,), jnp.int32),
        ),
        in_specs=[pl.BlockSpec(memory_space=pltpu.HBM)] * 9,
        out_specs=(anyw, pl.BlockSpec(memory_space=pltpu.VMEM), smem),
        scratch_shapes=scratch,
        compiler_params=pltpu.CompilerParams(
            collective_id=0, has_side_effects=True, vmem_limit_bytes=40 * 1024 * 1024
        ),
        cost_estimate=pl.CostEstimate(flops=2 * TOK * ROWS * COLS * LANES, bytes_accessed=6_000_000, transcendentals=0),
    )(live, keeper, former, target, features, og, st0, st1, st2)


def update_kernel(meta, states, grad, out_master, out_first, out_second):
    lane = lax.broadcasted_iota(jnp.int32, (WIN, LANES), 1)
    slot = lax.broadcasted_iota(jnp.int32, (WIN, LANES), 0) * LANES + lane
    begin, length = meta[0], meta[1]
    live = slot < length
    place = slot + begin

    def window(ref, row, shift):
        back = lax.rem(LANES - shift, LANES)
        here = pltpu.roll(ref[pl.ds(row, WIN), :], back, 1)
        after = pltpu.roll(ref[pl.ds(row + 1, WIN), :], back, 1)
        return jnp.where(lane < LANES - shift, here, after)

    delta = meta[2]
    row = jnp.clip(delta >> 7, 0, GRAD_ROWS - WIN - 1)
    gradient = jnp.where(live, window(grad, row, delta & 127), 0.0)

    gathered = [jnp.zeros((WIN, LANES), jnp.float32)] * 3
    for i in range(5):
        lower, upper = meta[3 + 2 * i], meta[4 + 2 * i]
        inside = (place >= lower) & (place < upper) & live
        delta = begin - lower
        row = jnp.clip(delta >> 7, -OUT_ROWS, OLD_ROWS)
        for a in range(3):
            base = (FRONT + 5 * a + i) * OLD_ROWS
            gathered[a] = jnp.where(inside, window(states, base + row, delta & 127), gathered[a])

    master, one, two = gathered
    first_next = BETA_ONE * one + (1.0 - BETA_ONE) * gradient
    second_next = BETA_TWO * two + (1.0 - BETA_TWO) * gradient * gradient
    update = first_next / CORRECT_ONE / (jnp.sqrt(second_next / CORRECT_TWO) + EPSILON)
    master_next = master - LEARN_RATE * (update + DECAY * master)
    for value, out in ((master_next, out_master), (first_next, out_first), (second_next, out_second)):
        value = jnp.where(live, value, 0.0)
        for t in range(OUT_ROWS):
            wide = min(LANES, NEW_CAP - t * LANES)
            out[:, t * LANES : t * LANES + wide] = value[t : t + 1, :wide]


def on_device(features, og, live, former, target, keeper, st0, st1, st2):
    states, grad, meta = gather_and_reduce(features, og, live, former, target, keeper, st0, st1, st2)
    states = states.reshape(SLOTS * OLD_ROWS, LANES)
    vm = pl.BlockSpec(memory_space=pltpu.VMEM)
    return pl.pallas_call(
        update_kernel,
        out_shape=[jax.ShapeDtypeStruct((1, NEW_CAP), jnp.float32)] * 3,
        in_specs=[pl.BlockSpec(memory_space=pltpu.SMEM), vm, vm],
        out_specs=[vm] * 3,
        compiler_params=pltpu.CompilerParams(vmem_limit_bytes=16 * 1024 * 1024),
        cost_estimate=pl.CostEstimate(flops=1_000_000, bytes_accessed=1_400_000, transcendentals=0),
    )(meta, states, grad)


def solution(mesh):
    placed = (
        P(("dp", "tensor"), None),
        P("dp", "tensor"),
        P(),
        P(),
        P(),
        P(),
        P("tensor", "dp"),
        P("tensor", "dp"),
        P("tensor", "dp"),
    )
    return jax.shard_map(
        on_device,
        mesh=mesh,
        in_specs=placed,
        out_specs=(P("tensor", "dp"), P("tensor", "dp"), P("tensor", "dp")),
        check_vma=False,
    )
```

```python
import functools
import jax
import jax.numpy as jnp
from jax import lax
from jax.experimental import pallas as pl
from jax.experimental.pallas import tpu as pltpu
from jax.sharding import PartitionSpec as P

BETA_ONE = 0.9
BETA_TWO = 0.95
EPSILON = 1e-08
DECAY = 0.1
LEARN_RATE = 0.02
CORRECT_ONE = 1.0 - 2.6561398887587544e-05
CORRECT_TWO = 1.0 - 0.005920529220333998

NX, NY, NC = 4, 8, 2
NDP = NX * NY * NC
NZ = 8
ROWS = 128
COLS = 28
TOK = 512
TOK_Z = TOK // NZ
LANES = 128
BLOCK = 7168
OLD_CAP = 12544
OLD_ROWS = OLD_CAP // LANES
NEW_CAP = 12659
OUT_ROWS = 99
WIN = 104
GRAD_ROWS = 304
SLOTS = 20
FRONT = 2
OFFSETS = (-2, -1, 1, 2)

CHUNKS = ((0, 12, "x"), (12, 8, "x"), (20, 8, "y"))


def slot_ids():
    row = lax.broadcasted_iota(jnp.int32, (WIN, LANES), 0)
    return row * LANES + lax.broadcasted_iota(jnp.int32, (WIN, LANES), 1)


def window(ref, row, shift):
    lane = lax.broadcasted_iota(jnp.int32, (WIN, LANES), 1)
    back = lax.rem(LANES - shift, LANES)
    here = pltpu.roll(ref[pl.ds(row, WIN), :], back, 1)
    after = pltpu.roll(ref[pl.ds(row + 1, WIN), :], back, 1)
    return jnp.where(lane < LANES - shift, here, after)


def main_kernel(
    live_in, keeper_in, former_in, target_in, feat, og, st0, st1, st2, slots, grad, meta,
    states, old, og_v, feat_all, mt, live, keeper, former, target, *rest,
):
    n = len(CHUNKS)
    part, core, r1, r2, fin = (rest[k * n : (k + 1) * n] for k in range(5))
    (ag_s, ag_r, og_sem, st_s, st_r, st_loc, co_s, co_r, s1_s, s1_r, s2_s, s2_r, rd_s, rd_r,
     in_sem) = rest[5 * n :]
    me = lax.axis_index("dp")
    z = lax.axis_index("tensor")
    c = lax.rem(me, NC)
    y = lax.rem(me // NC, NY)
    x = me // (NC * NY)

    def dp_of(x_, y_, c_):
        return (x_ * NY + y_) * NC + c_

    def dev(d, z_):
        return {"dp": d, "tensor": z_}

    def at_x(o):
        return dev(dp_of(lax.rem(x + o, NX), y, c), z)

    def at_y(o):
        return dev(dp_of(x, lax.rem(y + o, NY), c), z)

    def at_z(o):
        return dev(me, lax.rem(z + o, NZ))

    def at_d(o):
        return dev(lax.rem(me + o + NDP, NDP), z)

    sibling = dev(dp_of(x, y, 1 - c), z)

    my_rows = pl.ds(pl.multiple_of(z * TOK_Z, TOK_Z), TOK_Z)
    small = []
    for i, (a, b) in enumerate(
        ((keeper_in, keeper), (target_in, target), (former_in, former), (live_in, live),
         (feat, feat_all.at[my_rows]))
    ):
        small.append(pltpu.make_async_copy(a, b, in_sem.at[i]))
        small[-1].start()
    local = []
    for k, (j0, nj, _) in enumerate(CHUNKS):
        cols = pl.ds(j0 * LANES, nj * LANES)
        local.append(pltpu.make_async_copy(og.at[:, cols], og_v.at[:, cols], og_sem.at[k]))
        local[-1].start()
    mine = []
    for a, st in enumerate((st0, st1, st2)):
        mine.append(pltpu.make_async_copy(st, states.at[5 * a + 2], st_loc.at[a]))
        mine[-1].start()

    barrier = pltpu.get_barrier_semaphore()
    peers = (
        [at_z(o) for o in range(1, NZ)]
        + [sibling]
        + [at_x(o) for o in range(1, NX)]
        + [at_y(o) for o in range(1, NY)]
        + [at_d(o) for o in OFFSETS]
    )
    for p in peers:
        pl.semaphore_signal(barrier, inc=1, device_id=p, device_id_type=pl.DeviceIdType.MESH)
    pl.semaphore_wait(barrier, len(peers))

    sent = []

    def send(src, dst, s_sem, r_sem, to):
        copy = pltpu.make_async_remote_copy(
            src_ref=src, dst_ref=dst, send_sem=s_sem, recv_sem=r_sem,
            device_id=to, device_id_type=pl.DeviceIdType.MESH,
        )
        copy.start()
        sent.append(copy)
        return copy

    gather = [
        send(feat, feat_all.at[my_rows], ag_s.at[o - 1], ag_r.at[o - 1], at_z(o))
        for o in (4, 3, 5, 2, 6, 1, 7)
    ]

    moved = []
    for a, st in enumerate((st0, st1, st2)):
        for i, o in enumerate(OFFSETS):
            moved.append(
                send(st, states.at[5 * a + 2 - o], st_s.at[4 * a + i], st_r.at[4 * a + i], at_d(o))
            )

    for copy in small:
        copy.wait()

    def add_up(ref, count, stop):
        return lax.fori_loop(
            0, count, lambda i, t: t + jnp.where(i < stop, ref[i], 0), jnp.int32(0)
        )

    low = jnp.minimum(me, NDP - 2)
    high = jnp.maximum(me - 1, 0)
    at_same = (me < NDP - 1) & (keeper[low] == me)
    at_before = (me > 0) & (keeper[high] == me)
    owner = at_same | at_before
    cursor = jnp.where(at_same, low, high)
    begin = jnp.where(
        at_same, add_up(target, NDP - 1, low), add_up(target, NDP - 1, high)
    )
    length = jnp.where(owner, jnp.where(at_same, target[low], target[high]), 0)
    meta[0] = length
    meta[1] = begin - (me - 2) * BLOCK
    edges = []
    edge = add_up(former, NDP, me - 2)
    for i in range(5):
        s = me - 2 + i
        inside = (s >= 0) & (s < NDP)
        size = jnp.where(inside, former[jnp.clip(s, 0, NDP - 1)], 0)
        edges.append((edge, edge + size))
        edge = edge + size
    live_count = jnp.where(owner, live[me], 0)

    for copy in gather:
        copy.wait_recv()

    tok = lax.broadcasted_iota(jnp.int32, (TOK, ROWS), 0)
    masked = jnp.where(tok < live_count, feat_all[...].astype(jnp.float32), 0.0).astype(jnp.bfloat16)
    out_row = lax.broadcasted_iota(jnp.int32, (ROWS, ROWS), 0)
    in_row = lax.broadcasted_iota(jnp.int32, (ROWS, ROWS), 1)
    for w, order in enumerate(("x", "y")):
        cc, b, i = out_row // 64, lax.rem(out_row // 2, 32), lax.rem(out_row, 2)
        if order == "x":
            bx, by = b // NY, lax.rem(b, NY)
        else:
            bx, by = lax.rem(b, NX), b // NX
        pick = (in_row == ((bx * NY + by) * NC + cc) * 2 + i).astype(jnp.float32).astype(jnp.bfloat16)
        mt[w] = lax.dot_general(
            pick, masked, (((1,), (1,)), ((), ())), preferred_element_type=jnp.float32
        ).astype(jnp.bfloat16)

    cores = []
    for k, (j0, nj, order) in enumerate(CHUNKS):
        local[k].wait()
        w = 0 if order == "x" else 1
        for j in range(0, nj, 2):
            out = jnp.dot(
                mt[w],
                og_v[:, (j0 + j) * LANES : (j0 + j + 2) * LANES],
                preferred_element_type=jnp.float32,
            )
            part[k][pl.ds(j, ROWS, stride=nj), :] = out[:, :LANES]
            part[k][pl.ds(j + 1, ROWS, stride=nj), :] = out[:, LANES:]
        half = 64 * nj
        cores.append(
            send(
                part[k].at[pl.ds(pl.multiple_of((1 - c) * half, half), half)],
                core[k], co_s.at[k], co_r.at[k], sibling,
            )
        )

    def plan(order):
        if order == "x":
            return NX, x, at_x, NY, y, at_y
        return NY, y, at_y, NX, x, at_x

    first = []
    for k, (j0, nj, order) in enumerate(CHUNKS):
        n1, i1, at1, n2, i2, at2 = plan(order)
        g1 = 64 * nj // n1
        half = 64 * nj
        cores[k].wait_recv()
        copies = []
        for o in list(range(1, n1)) + [0]:
            row = pl.multiple_of(lax.rem(i1 + o, n1) * g1, g1)
            core[k][pl.ds(row, g1)] = core[k][pl.ds(row, g1)] + part[k][pl.ds(pl.multiple_of(c * half + row, g1), g1)]
            if o:
                copies.append(
                    send(core[k].at[pl.ds(row, g1)], r1[k].at[pl.ds((o - 1) * g1, g1)],
                         s1_s.at[k, o - 1], s1_r.at[k, o - 1], at1(o))
                )
        first.append(copies)

    for copy in mine:
        copy.wait()
    for copy in moved:
        copy.wait_recv()
    for i in range(15):
        first_row = (FRONT + i) * OLD_ROWS
        old[first_row : first_row + OLD_ROWS] = states[i].reshape(OLD_ROWS, LANES)
    slot = slot_ids()
    place = slot + begin
    gathered = [jnp.zeros((WIN, LANES), jnp.float32)] * 3
    for i, (lower, upper) in enumerate(edges):
        inside = (place >= lower) & (place < upper) & (slot < length)
        delta = begin - lower
        row = jnp.clip(delta >> 7, -OUT_ROWS, OLD_ROWS)
        for a in range(3):
            base = (FRONT + 5 * a + i) * OLD_ROWS
            gathered[a] = jnp.where(inside, window(old, base + row, delta & 127), gathered[a])
    for a in range(3):
        slots[a * WIN : (a + 1) * WIN] = gathered[a]

    second = []
    for k, (j0, nj, order) in enumerate(CHUNKS):
        n1, i1, at1, n2, i2, at2 = plan(order)
        g1 = 64 * nj // n1
        g2 = 2 * nj
        for copy in first[k]:
            copy.wait_recv()
        copies = []
        for o in list(range(1, n2)) + [0]:
            row = pl.multiple_of(lax.rem(i2 + o, n2) * g2, g2)
            base = pl.multiple_of(i1 * g1 + row, g2)
            total = core[k][pl.ds(base, g2)]
            for q in range(n1 - 1):
                total = total + r1[k][pl.ds(pl.multiple_of(q * g1 + row, g2), g2)]
            spot = pl.ds(pl.multiple_of(c * 64 * nj + row, g2), g2)
            part[k][spot] = total
            if o:
                copies.append(
                    send(part[k].at[spot], r2[k].at[pl.ds((o - 1) * g2, g2)],
                         s2_s.at[k, o - 1], s2_r.at[k, o - 1], at2(o))
                )
        second.append(copies)

    third = []
    for k, (j0, nj, order) in enumerate(CHUNKS):
        n1, i1, at1, n2, i2, at2 = plan(order)
        g2 = 2 * nj
        for copy in second[k]:
            copy.wait_recv()
        total = part[k][pl.ds(pl.multiple_of(c * 64 * nj + i2 * g2, g2), g2)]
        for q in range(n2 - 1):
            total = total + r2[k][q * g2 : (q + 1) * g2]
        fin[k][2 * g2 : 3 * g2] = total
        third.append([
            send(fin[k].at[pl.ds(2 * g2, g2)], fin[k].at[pl.ds((2 - o) * g2, g2)],
                 rd_s.at[k, i], rd_r.at[k, i], at_d(o))
            for i, o in enumerate(OFFSETS)
        ])

    for k, (j0, nj, order) in enumerate(CHUNKS):
        for copy in third[k]:
            copy.wait_recv()
        for m in range(10):
            grad[m * COLS + j0 : m * COLS + j0 + nj] = fin[k][m * nj : (m + 1) * nj]

    for copy in sent:
        copy.wait_send()


def gather_and_reduce(features, og, live, former, target, keeper, st0, st1, st2):
    n = len(CHUNKS)
    vmem = lambda rows, dtype=jnp.float32: pltpu.VMEM((rows, LANES), dtype)
    scratch = [
        pltpu.VMEM((15, 1, OLD_CAP), jnp.float32),
        vmem(SLOTS * OLD_ROWS),
        pltpu.VMEM((TOK, COLS * LANES), jnp.bfloat16),
        vmem(TOK, jnp.bfloat16),
        pltpu.VMEM((2, ROWS, TOK), jnp.bfloat16),
    ] + [pltpu.SMEM(v.shape, jnp.int32) for v in (live, keeper, former, target)]
    counts = [(NX, NY) if order == "x" else (NY, NX) for _, _, order in CHUNKS]
    scratch += [vmem(ROWS * nj) for _, nj, _ in CHUNKS]
    scratch += [vmem(64 * nj) for _, nj, _ in CHUNKS]
    scratch += [vmem((n1 - 1) * 64 * nj // n1) for (_, nj, _), (n1, n2) in zip(CHUNKS, counts)]
    scratch += [vmem((n2 - 1) * 2 * nj) for (_, nj, _), (n1, n2) in zip(CHUNKS, counts)]
    scratch += [vmem(10 * nj) for _, nj, _ in CHUNKS]
    dma = lambda *s: pltpu.SemaphoreType.DMA(s)
    scratch += [
        dma(7), dma(7), dma(n), dma(12), dma(12), dma(3), dma(n), dma(n),
        dma(n, 7), dma(n, 7), dma(n, 7), dma(n, 7), dma(n, 4), dma(n, 4), dma(5),
    ]
    smem = pl.BlockSpec(memory_space=pltpu.SMEM)
    vm = pl.BlockSpec(memory_space=pltpu.VMEM)
    return pl.pallas_call(
        main_kernel,
        out_shape=(
            jax.ShapeDtypeStruct((3 * WIN, LANES), jnp.float32),
            jax.ShapeDtypeStruct((GRAD_ROWS, LANES), jnp.float32),
            jax.ShapeDtypeStruct((2,), jnp.int32),
        ),
        in_specs=[pl.BlockSpec(memory_space=pltpu.HBM)] * 9,
        out_specs=(vm, vm, smem),
        scratch_shapes=scratch,
        compiler_params=pltpu.CompilerParams(
            collective_id=0, has_side_effects=True, vmem_limit_bytes=56 * 1024 * 1024
        ),
        cost_estimate=pl.CostEstimate(flops=2 * TOK * ROWS * COLS * LANES, bytes_accessed=6_000_000, transcendentals=0),
    )(live, keeper, former, target, features, og, st0, st1, st2)


def update_kernel(
    meta_in, slots_in, grad_in, out_master, out_first, out_second, meta, slots, grad, sem
):
    copies = [
        pltpu.make_async_copy(a, b, sem.at[i])
        for i, (a, b) in enumerate(((meta_in, meta), (slots_in, slots), (grad_in, grad)))
    ]
    for copy in copies:
        copy.start()
    for copy in copies:
        copy.wait()
    live = slot_ids() < meta[0]
    delta = meta[1]
    row = jnp.clip(delta >> 7, 0, GRAD_ROWS - WIN - 1)
    gradient = jnp.where(live, window(grad, row, delta & 127), 0.0)
    master, one, two = (slots[a * WIN : (a + 1) * WIN] for a in range(3))
    first_next = BETA_ONE * one + (1.0 - BETA_ONE) * gradient
    second_next = BETA_TWO * two + (1.0 - BETA_TWO) * gradient * gradient
    update = first_next / CORRECT_ONE / (jnp.sqrt(second_next / CORRECT_TWO) + EPSILON)
    master_next = master - LEARN_RATE * (update + DECAY * master)
    for value, out in ((master_next, out_master), (first_next, out_first), (second_next, out_second)):
        value = jnp.where(live, value, 0.0)
        for t in range(OUT_ROWS):
            wide = min(LANES, NEW_CAP - t * LANES)
            out[:, t * LANES : t * LANES + wide] = value[t : t + 1, :wide]


def on_device(features, og, live, former, target, keeper, st0, st1, st2):
    slots, grad, meta = gather_and_reduce(features, og, live, former, target, keeper, st0, st1, st2)
    vm = pl.BlockSpec(memory_space=pltpu.VMEM)
    return pl.pallas_call(
        update_kernel,
        out_shape=[jax.ShapeDtypeStruct((1, NEW_CAP), jnp.float32)] * 3,
        in_specs=[pl.BlockSpec(memory_space=pl.ANY)] * 3,
        out_specs=[vm] * 3,
        scratch_shapes=[
            pltpu.SMEM(meta.shape, meta.dtype),
            pltpu.VMEM(slots.shape, slots.dtype),
            pltpu.VMEM(grad.shape, grad.dtype),
            pltpu.SemaphoreType.DMA((3,)),
        ],
        compiler_params=pltpu.CompilerParams(vmem_limit_bytes=56 * 1024 * 1024),
        cost_estimate=pl.CostEstimate(flops=1_000_000, bytes_accessed=1_400_000, transcendentals=0),
    )(meta, slots, grad)


def solution(mesh):
    placed = (
        P(("dp", "tensor"), None),
        P("dp", "tensor"),
        P(),
        P(),
        P(),
        P(),
        P("tensor", "dp"),
        P("tensor", "dp"),
        P("tensor", "dp"),
    )
    return jax.shard_map(
        on_device,
        mesh=mesh,
        in_specs=placed,
        out_specs=(P("tensor", "dp"), P("tensor", "dp"), P("tensor", "dp")),
        check_vma=False,
    )
```

```python
import functools
import jax
import jax.numpy as jnp
from jax import lax
from jax.experimental import pallas as pl
from jax.experimental.pallas import tpu as pltpu
from jax.sharding import PartitionSpec as P

BETA_ONE = 0.9
BETA_TWO = 0.95
EPSILON = 1e-08
DECAY = 0.1
LEARN_RATE = 0.02
CORRECT_ONE = 1.0 - 2.6561398887587544e-05
CORRECT_TWO = 1.0 - 0.005920529220333998

NX, NY, NC = 4, 8, 2
NDP = NX * NY * NC
NZ = 8
ROWS = 128
COLS = 28
TOK = 512
TOK_Z = TOK // NZ
LANES = 128
BLOCK = 7168
OLD_CAP = 12544
OLD_ROWS = OLD_CAP // LANES
NEW_CAP = 12659
OUT_ROWS = 99
WIN = 104
GRAD_ROWS = 304
SLOTS = 20
FRONT = 2
OFFSETS = (-2, -1, 1, 2)

CHUNKS = ((0, 12, "x"), (12, 8, "x"), (20, 8, "y"))


def slot_ids():
    row = lax.broadcasted_iota(jnp.int32, (WIN, LANES), 0)
    return row * LANES + lax.broadcasted_iota(jnp.int32, (WIN, LANES), 1)


def window(ref, row, shift):
    lane = lax.broadcasted_iota(jnp.int32, (WIN, LANES), 1)
    back = lax.rem(LANES - shift, LANES)
    here = pltpu.roll(ref[pl.ds(row, WIN), :], back, 1)
    after = pltpu.roll(ref[pl.ds(row + 1, WIN), :], back, 1)
    return jnp.where(lane < LANES - shift, here, after)


def main_kernel(
    live_in, keeper_in, former_in, target_in, feat, og, st0, st1, st2, slots,
    states, old, kept, grad, pick, og_v, feat_all, mt, live, keeper, former, target, *rest,
):
    n = len(CHUNKS)
    part, core, r1, r2, fin = (rest[k * n : (k + 1) * n] for k in range(5))
    (ag_s, ag_r, og_sem, st_s, st_r, st_loc, co_s, co_r, s1_s, s1_r, s2_s, s2_r, rd_s, rd_r,
     in_sem) = rest[5 * n :]
    me = lax.axis_index("dp")
    z = lax.axis_index("tensor")
    c = lax.rem(me, NC)
    y = lax.rem(me // NC, NY)
    x = me // (NC * NY)

    def dp_of(x_, y_, c_):
        return (x_ * NY + y_) * NC + c_

    def dev(d, z_):
        return {"dp": d, "tensor": z_}

    def at_x(o):
        return dev(dp_of(lax.rem(x + o, NX), y, c), z)

    def at_y(o):
        return dev(dp_of(x, lax.rem(y + o, NY), c), z)

    def at_z(o):
        return dev(me, lax.rem(z + o, NZ))

    def at_d(o):
        return dev(lax.rem(me + o + NDP, NDP), z)

    sibling = dev(dp_of(x, y, 1 - c), z)

    barrier = pltpu.get_barrier_semaphore()
    peers = (
        [at_z(o) for o in range(1, NZ)]
        + [sibling]
        + [at_x(o) for o in range(1, NX)]
        + [at_y(o) for o in range(1, NY)]
        + [at_d(o) for o in OFFSETS]
    )
    for p in peers:
        pl.semaphore_signal(barrier, inc=1, device_id=p, device_id_type=pl.DeviceIdType.MESH)
    my_rows = pl.ds(pl.multiple_of(z * TOK_Z, TOK_Z), TOK_Z)
    small = []
    for i, (a, b) in enumerate(
        ((keeper_in, keeper), (target_in, target), (former_in, former), (live_in, live),
         (feat, feat_all.at[my_rows]))
    ):
        small.append(pltpu.make_async_copy(a, b, in_sem.at[i]))
        small[-1].start()
    local = []
    for k, (j0, nj, _) in enumerate(CHUNKS):
        cols = pl.ds(j0 * LANES, nj * LANES)
        local.append(pltpu.make_async_copy(og.at[:, cols], og_v.at[:, cols], og_sem.at[k]))
        local[-1].start()
    mine = []
    for a, st in enumerate((st0, st1, st2)):
        mine.append(pltpu.make_async_copy(st, states.at[5 * a + 2], st_loc.at[a]))
        mine[-1].start()

    pl.semaphore_wait(barrier, len(peers))

    sent = []

    def send(src, dst, s_sem, r_sem, to):
        copy = pltpu.make_async_remote_copy(
            src_ref=src, dst_ref=dst, send_sem=s_sem, recv_sem=r_sem,
            device_id=to, device_id_type=pl.DeviceIdType.MESH,
        )
        copy.start()
        sent.append(copy)
        return copy

    gather = [
        send(feat, feat_all.at[my_rows], ag_s.at[o - 1], ag_r.at[o - 1], at_z(o))
        for o in (4, 3, 5, 2, 6, 1, 7)
    ]

    moved = []
    for a, st in enumerate((st0, st1, st2)):
        for i, o in enumerate(OFFSETS):
            moved.append(
                send(st, states.at[5 * a + 2 - o], st_s.at[4 * a + i], st_r.at[4 * a + i], at_d(o))
            )

    for copy in small:
        copy.wait()

    def add_up(ref, count, stop):
        return lax.fori_loop(
            0, count, lambda i, t: t + jnp.where(i < stop, ref[i], 0), jnp.int32(0)
        )

    low = jnp.minimum(me, NDP - 2)
    high = jnp.maximum(me - 1, 0)
    at_same = (me < NDP - 1) & (keeper[low] == me)
    at_before = (me > 0) & (keeper[high] == me)
    owner = at_same | at_before
    cursor = jnp.where(at_same, low, high)
    begin = jnp.where(
        at_same, add_up(target, NDP - 1, low), add_up(target, NDP - 1, high)
    )
    length = jnp.where(owner, jnp.where(at_same, target[low], target[high]), 0)
    edges = []
    edge = add_up(former, NDP, me - 2)
    for i in range(5):
        s = me - 2 + i
        inside = (s >= 0) & (s < NDP)
        size = jnp.where(inside, former[jnp.clip(s, 0, NDP - 1)], 0)
        edges.append((edge, edge + size))
        edge = edge + size
    live_count = jnp.where(owner, live[me], 0)

    out_row = lax.broadcasted_iota(jnp.int32, (ROWS, ROWS), 0)
    in_row = lax.broadcasted_iota(jnp.int32, (ROWS, ROWS), 1)
    for w, order in enumerate(("x", "y")):
        cc, b, i = out_row // 64, lax.rem(out_row // 2, 32), lax.rem(out_row, 2)
        if order == "x":
            bx, by = b // NY, lax.rem(b, NY)
        else:
            bx, by = lax.rem(b, NX), b // NX
        pick[w] = (in_row == ((bx * NY + by) * NC + cc) * 2 + i).astype(jnp.float32).astype(jnp.bfloat16)

    for copy in gather:
        copy.wait_recv()

    tok = lax.broadcasted_iota(jnp.int32, (TOK, ROWS), 0)
    masked = jnp.where(tok < live_count, feat_all[...].astype(jnp.float32), 0.0).astype(jnp.bfloat16)
    for w in range(2):
        mt[w] = lax.dot_general(
            pick[w], masked, (((1,), (1,)), ((), ())), preferred_element_type=jnp.float32
        ).astype(jnp.bfloat16)

    cores = []
    for k, (j0, nj, order) in enumerate(CHUNKS):
        local[k].wait()
        w = 0 if order == "x" else 1
        for j in range(0, nj, 2):
            out = jnp.dot(
                mt[w],
                og_v[:, (j0 + j) * LANES : (j0 + j + 2) * LANES],
                preferred_element_type=jnp.float32,
            )
            part[k][pl.ds(j, ROWS, stride=nj), :] = out[:, :LANES]
            part[k][pl.ds(j + 1, ROWS, stride=nj), :] = out[:, LANES:]
        half = 64 * nj
        cores.append(
            send(
                part[k].at[pl.ds(pl.multiple_of((1 - c) * half, half), half)],
                core[k], co_s.at[k], co_r.at[k], sibling,
            )
        )

    def plan(order):
        if order == "x":
            return NX, x, at_x, NY, y, at_y
        return NY, y, at_y, NX, x, at_x

    first = []
    for k, (j0, nj, order) in enumerate(CHUNKS):
        n1, i1, at1, n2, i2, at2 = plan(order)
        g1 = 64 * nj // n1
        half = 64 * nj
        cores[k].wait_recv()
        copies = []
        for o in list(range(1, n1)) + [0]:
            row = pl.multiple_of(lax.rem(i1 + o, n1) * g1, g1)
            core[k][pl.ds(row, g1)] = core[k][pl.ds(row, g1)] + part[k][pl.ds(pl.multiple_of(c * half + row, g1), g1)]
            if o:
                copies.append(
                    send(core[k].at[pl.ds(row, g1)], r1[k].at[pl.ds((o - 1) * g1, g1)],
                         s1_s.at[k, o - 1], s1_r.at[k, o - 1], at1(o))
                )
        first.append(copies)

    for copy in mine:
        copy.wait()
    for copy in moved:
        copy.wait_recv()
    for i in range(15):
        first_row = (FRONT + i) * OLD_ROWS
        old[first_row : first_row + OLD_ROWS] = states[i].reshape(OLD_ROWS, LANES)
    slot = slot_ids()
    place = slot + begin
    gathered = [jnp.zeros((WIN, LANES), jnp.float32)] * 3
    for i, (lower, upper) in enumerate(edges):
        inside = (place >= lower) & (place < upper) & (slot < length)
        delta = begin - lower
        row = jnp.clip(delta >> 7, -OUT_ROWS, OLD_ROWS)
        for a in range(3):
            base = (FRONT + 5 * a + i) * OLD_ROWS
            gathered[a] = jnp.where(inside, window(old, base + row, delta & 127), gathered[a])
    for a in range(3):
        kept[a] = gathered[a]

    second = []
    for k, (j0, nj, order) in enumerate(CHUNKS):
        n1, i1, at1, n2, i2, at2 = plan(order)
        g1 = 64 * nj // n1
        g2 = 2 * nj
        for copy in first[k]:
            copy.wait_recv()
        copies = []
        for o in list(range(1, n2)) + [0]:
            row = pl.multiple_of(lax.rem(i2 + o, n2) * g2, g2)
            base = pl.multiple_of(i1 * g1 + row, g2)
            total = core[k][pl.ds(base, g2)]
            for q in range(n1 - 1):
                total = total + r1[k][pl.ds(pl.multiple_of(q * g1 + row, g2), g2)]
            spot = pl.ds(pl.multiple_of(c * 64 * nj + row, g2), g2)
            part[k][spot] = total
            if o:
                copies.append(
                    send(part[k].at[spot], r2[k].at[pl.ds((o - 1) * g2, g2)],
                         s2_s.at[k, o - 1], s2_r.at[k, o - 1], at2(o))
                )
        second.append(copies)

    third = []
    for k, (j0, nj, order) in enumerate(CHUNKS):
        n1, i1, at1, n2, i2, at2 = plan(order)
        g2 = 2 * nj
        for copy in second[k]:
            copy.wait_recv()
        total = part[k][pl.ds(pl.multiple_of(c * 64 * nj + i2 * g2, g2), g2)]
        for q in range(n2 - 1):
            total = total + r2[k][q * g2 : (q + 1) * g2]
        fin[k][2 * g2 : 3 * g2] = total
        third.append([
            send(fin[k].at[pl.ds(2 * g2, g2)], fin[k].at[pl.ds((2 - o) * g2, g2)],
                 rd_s.at[k, i], rd_r.at[k, i], at_d(o))
            for i, o in enumerate(OFFSETS)
        ])

    for k, (j0, nj, order) in enumerate(CHUNKS):
        for copy in third[k]:
            copy.wait_recv()
        for m in range(10):
            grad[m * COLS + j0 : m * COLS + j0 + nj] = fin[k][m * nj : (m + 1) * nj]

    live_slot = slot_ids() < length
    delta = begin - (me - 2) * BLOCK
    row = jnp.clip(delta >> 7, 0, GRAD_ROWS - WIN - 1)
    gradient = jnp.where(live_slot, window(grad, row, delta & 127), 0.0)
    master, one, two = kept[0], kept[1], kept[2]
    first_next = BETA_ONE * one + (1.0 - BETA_ONE) * gradient
    second_next = BETA_TWO * two + (1.0 - BETA_TWO) * gradient * gradient
    update = first_next / CORRECT_ONE / (jnp.sqrt(second_next / CORRECT_TWO) + EPSILON)
    master_next = master - LEARN_RATE * (update + DECAY * master)
    for a, value in enumerate((master_next, first_next, second_next)):
        slots[a * WIN : (a + 1) * WIN] = jnp.where(live_slot, value, 0.0)

    for copy in sent:
        copy.wait_send()


def gather_and_reduce(features, og, live, former, target, keeper, st0, st1, st2):
    n = len(CHUNKS)
    vmem = lambda rows, dtype=jnp.float32: pltpu.VMEM((rows, LANES), dtype)
    scratch = [
        pltpu.VMEM((15, 1, OLD_CAP), jnp.float32),
        vmem(SLOTS * OLD_ROWS),
        pltpu.VMEM((3, WIN, LANES), jnp.float32),
        vmem(GRAD_ROWS),
        pltpu.VMEM((2, ROWS, ROWS), jnp.bfloat16),
        pltpu.VMEM((TOK, COLS * LANES), jnp.bfloat16),
        vmem(TOK, jnp.bfloat16),
        pltpu.VMEM((2, ROWS, TOK), jnp.bfloat16),
    ] + [pltpu.SMEM(v.shape, jnp.int32) for v in (live, keeper, former, target)]
    counts = [(NX, NY) if order == "x" else (NY, NX) for _, _, order in CHUNKS]
    scratch += [vmem(ROWS * nj) for _, nj, _ in CHUNKS]
    scratch += [vmem(64 * nj) for _, nj, _ in CHUNKS]
    scratch += [vmem((n1 - 1) * 64 * nj // n1) for (_, nj, _), (n1, n2) in zip(CHUNKS, counts)]
    scratch += [vmem((n2 - 1) * 2 * nj) for (_, nj, _), (n1, n2) in zip(CHUNKS, counts)]
    scratch += [vmem(10 * nj) for _, nj, _ in CHUNKS]
    dma = lambda *s: pltpu.SemaphoreType.DMA(s)
    scratch += [
        dma(7), dma(7), dma(n), dma(12), dma(12), dma(3), dma(n), dma(n),
        dma(n, 7), dma(n, 7), dma(n, 7), dma(n, 7), dma(n, 4), dma(n, 4), dma(5),
    ]
    vm = pl.BlockSpec(memory_space=pltpu.VMEM)
    return pl.pallas_call(
        main_kernel,
        out_shape=jax.ShapeDtypeStruct((3 * WIN, LANES), jnp.float32),
        in_specs=[pl.BlockSpec(memory_space=pltpu.HBM)] * 9,
        out_specs=vm,
        scratch_shapes=scratch,
        compiler_params=pltpu.CompilerParams(
            collective_id=0, has_side_effects=True, vmem_limit_bytes=56 * 1024 * 1024
        ),
        cost_estimate=pl.CostEstimate(flops=2 * TOK * ROWS * COLS * LANES, bytes_accessed=6_000_000, transcendentals=0),
    )(live, keeper, former, target, features, og, st0, st1, st2)


def lay_out_kernel(slots_in, out_master, out_first, out_second, slots, sem):
    copies = [
        pltpu.make_async_copy(slots_in.at[pl.ds(a * WIN, WIN)], slots.at[a], sem.at[a]) for a in range(3)
    ]
    for copy in copies:
        copy.start()
    for copy, a, out in zip(copies, range(3), (out_master, out_first, out_second)):
        copy.wait()
        value = slots[a]
        for t in range(OUT_ROWS):
            wide = min(LANES, NEW_CAP - t * LANES)
            out[:, t * LANES : t * LANES + wide] = value[t : t + 1, :wide]


def on_device(features, og, live, former, target, keeper, st0, st1, st2):
    slots = gather_and_reduce(features, og, live, former, target, keeper, st0, st1, st2)
    vm = pl.BlockSpec(memory_space=pltpu.VMEM)
    return pl.pallas_call(
        lay_out_kernel,
        out_shape=[jax.ShapeDtypeStruct((1, NEW_CAP), jnp.float32)] * 3,
        in_specs=[pl.BlockSpec(memory_space=pl.ANY)],
        out_specs=[vm] * 3,
        scratch_shapes=[
            pltpu.VMEM((3, WIN, LANES), jnp.float32),
            pltpu.SemaphoreType.DMA((3,)),
        ],
        compiler_params=pltpu.CompilerParams(vmem_limit_bytes=56 * 1024 * 1024),
        cost_estimate=pl.CostEstimate(flops=100_000, bytes_accessed=320_000, transcendentals=0),
    )(slots)


def solution(mesh):
    placed = (
        P(("dp", "tensor"), None),
        P("dp", "tensor"),
        P(),
        P(),
        P(),
        P(),
        P("tensor", "dp"),
        P("tensor", "dp"),
        P("tensor", "dp"),
    )
    return jax.shard_map(
        on_device,
        mesh=mesh,
        in_specs=placed,
        out_specs=(P("tensor", "dp"), P("tensor", "dp"), P("tensor", "dp")),
        check_vma=False,
    )
```

```python
import functools
import jax
import jax.numpy as jnp
from jax import lax
from jax.experimental import pallas as pl
from jax.experimental.pallas import tpu as pltpu
from jax.sharding import PartitionSpec as P

BETA_ONE = 0.9
BETA_TWO = 0.95
EPSILON = 1e-08
DECAY = 0.1
LEARN_RATE = 0.02
CORRECT_ONE = 1.0 - 2.6561398887587544e-05
CORRECT_TWO = 1.0 - 0.005920529220333998

NX, NY, NC = 4, 8, 2
NDP = NX * NY * NC
NZ = 8
ROWS = 128
COLS = 28
TOK = 512
TOK_Z = TOK // NZ
LANES = 128
BLOCK = 7168
OLD_CAP = 12544
OLD_ROWS = OLD_CAP // LANES
NEW_CAP = 12659
OUT_ROWS = 99
WIN = 104
GRAD_ROWS = 304
SLOTS = 20
FRONT = 2
OFFSETS = (-2, -1, 1, 2)

CHUNKS = ((0, 12, "x"), (12, 8, "y"), (20, 8, "x"))


def slot_ids():
    row = lax.broadcasted_iota(jnp.int32, (WIN, LANES), 0)
    return row * LANES + lax.broadcasted_iota(jnp.int32, (WIN, LANES), 1)


def window(ref, row, shift):
    lane = lax.broadcasted_iota(jnp.int32, (WIN, LANES), 1)
    back = lax.rem(LANES - shift, LANES)
    here = pltpu.roll(ref[pl.ds(row, WIN), :], back, 1)
    after = pltpu.roll(ref[pl.ds(row + 1, WIN), :], back, 1)
    return jnp.where(lane < LANES - shift, here, after)


def main_kernel(
    live_in, keeper_in, former_in, target_in, feat, og, st0, st1, st2, slots,
    states, old, kept, grad, pick, og_v, feat_all, mt, live, keeper, former, target, *rest,
):
    n = len(CHUNKS)
    part, core, r1, r2, fin = (rest[k * n : (k + 1) * n] for k in range(5))
    (ag_s, ag_r, og_sem, st_s, st_r, st_loc, co_s, co_r, s1_s, s1_r, s2_s, s2_r, rd_s, rd_r,
     in_sem) = rest[5 * n :]
    me = lax.axis_index("dp")
    z = lax.axis_index("tensor")
    c = lax.rem(me, NC)
    y = lax.rem(me // NC, NY)
    x = me // (NC * NY)

    def dp_of(x_, y_, c_):
        return (x_ * NY + y_) * NC + c_

    def dev(d, z_):
        return {"dp": d, "tensor": z_}

    def at_x(o):
        return dev(dp_of(lax.rem(x + o, NX), y, c), z)

    def at_y(o):
        return dev(dp_of(x, lax.rem(y + o, NY), c), z)

    def at_z(o):
        return dev(me, lax.rem(z + o, NZ))

    def at_d(o):
        return dev(lax.rem(me + o + NDP, NDP), z)

    sibling = dev(dp_of(x, y, 1 - c), z)

    barrier = pltpu.get_barrier_semaphore()
    peers = (
        [at_z(o) for o in range(1, NZ)]
        + [sibling]
        + [at_x(o) for o in range(1, NX)]
        + [at_y(o) for o in range(1, NY)]
        + [at_d(o) for o in OFFSETS]
    )
    for p in peers:
        pl.semaphore_signal(barrier, inc=1, device_id=p, device_id_type=pl.DeviceIdType.MESH)
    my_rows = pl.ds(pl.multiple_of(z * TOK_Z, TOK_Z), TOK_Z)
    small = []
    for i, (a, b) in enumerate(
        ((keeper_in, keeper), (target_in, target), (former_in, former), (live_in, live),
         (feat, feat_all.at[my_rows]))
    ):
        small.append(pltpu.make_async_copy(a, b, in_sem.at[i]))
        small[-1].start()
    local = []
    for k, (j0, nj, _) in enumerate(CHUNKS):
        cols = pl.ds(j0 * LANES, nj * LANES)
        local.append(pltpu.make_async_copy(og.at[:, cols], og_v.at[:, cols], og_sem.at[k]))
        local[-1].start()
    mine = []
    for a, st in enumerate((st0, st1, st2)):
        mine.append(pltpu.make_async_copy(st, states.at[5 * a + 2], st_loc.at[a]))
        mine[-1].start()

    pl.semaphore_wait(barrier, len(peers))

    sent = []

    def send(src, dst, s_sem, r_sem, to):
        copy = pltpu.make_async_remote_copy(
            src_ref=src, dst_ref=dst, send_sem=s_sem, recv_sem=r_sem,
            device_id=to, device_id_type=pl.DeviceIdType.MESH,
        )
        copy.start()
        sent.append(copy)
        return copy

    gather = [
        send(feat, feat_all.at[my_rows], ag_s.at[o - 1], ag_r.at[o - 1], at_z(o))
        for o in (4, 3, 5, 2, 6, 1, 7)
    ]

    moved = []
    for a, st in enumerate((st0, st1, st2)):
        for i, o in enumerate(OFFSETS):
            moved.append(
                send(st, states.at[5 * a + 2 - o], st_s.at[4 * a + i], st_r.at[4 * a + i], at_d(o))
            )

    for copy in small:
        copy.wait()

    def add_up(ref, count, stop):
        return lax.fori_loop(
            0, count, lambda i, t: t + jnp.where(i < stop, ref[i], 0), jnp.int32(0)
        )

    low = jnp.minimum(me, NDP - 2)
    high = jnp.maximum(me - 1, 0)
    at_same = (me < NDP - 1) & (keeper[low] == me)
    at_before = (me > 0) & (keeper[high] == me)
    owner = at_same | at_before
    cursor = jnp.where(at_same, low, high)
    begin = jnp.where(
        at_same, add_up(target, NDP - 1, low), add_up(target, NDP - 1, high)
    )
    length = jnp.where(owner, jnp.where(at_same, target[low], target[high]), 0)
    edges = []
    edge = add_up(former, NDP, me - 2)
    for i in range(5):
        s = me - 2 + i
        inside = (s >= 0) & (s < NDP)
        size = jnp.where(inside, former[jnp.clip(s, 0, NDP - 1)], 0)
        edges.append((edge, edge + size))
        edge = edge + size
    live_count = jnp.where(owner, live[me], 0)

    out_row = lax.broadcasted_iota(jnp.int32, (ROWS, ROWS), 0)
    in_row = lax.broadcasted_iota(jnp.int32, (ROWS, ROWS), 1)
    for w, order in enumerate(("x", "y")):
        cc, b, i = out_row // 64, lax.rem(out_row // 2, 32), lax.rem(out_row, 2)
        if order == "x":
            bx, by = b // NY, lax.rem(b, NY)
        else:
            bx, by = lax.rem(b, NX), b // NX
        pick[w] = (in_row == ((bx * NY + by) * NC + cc) * 2 + i).astype(jnp.float32).astype(jnp.bfloat16)

    for copy in gather:
        copy.wait_recv()

    tok = lax.broadcasted_iota(jnp.int32, (TOK, ROWS), 0)
    masked = jnp.where(tok < live_count, feat_all[...].astype(jnp.float32), 0.0).astype(jnp.bfloat16)
    def reorder(w):
        mt[w] = lax.dot_general(
            pick[w], masked, (((1,), (1,)), ((), ())), preferred_element_type=jnp.float32
        ).astype(jnp.bfloat16)

    reorder(0)
    reorder(1)
    def plan(order):
        if order == "x":
            return NX, x, at_x, NY, y, at_y
        return NY, y, at_y, NX, x, at_x

    cores, first = [], []

    def multiply(k):
        j0, nj, order = CHUNKS[k]
        local[k].wait()
        w = 0 if order == "x" else 1
        for j in range(0, nj, 2):
            out = jnp.dot(
                mt[w],
                og_v[:, (j0 + j) * LANES : (j0 + j + 2) * LANES],
                preferred_element_type=jnp.float32,
            )
            part[k][pl.ds(j, ROWS, stride=nj), :] = out[:, :LANES]
            part[k][pl.ds(j + 1, ROWS, stride=nj), :] = out[:, LANES:]
        half = 64 * nj
        cores.append(
            send(
                part[k].at[pl.ds(pl.multiple_of((1 - c) * half, half), half)],
                core[k], co_s.at[k], co_r.at[k], sibling,
            )
        )

    def begin_first(k):
        j0, nj, order = CHUNKS[k]
        n1, i1, at1, n2, i2, at2 = plan(order)
        g1 = 64 * nj // n1
        half = 64 * nj
        cores[k].wait_recv()
        copies = []
        for o in list(range(1, n1)) + [0]:
            row = pl.multiple_of(lax.rem(i1 + o, n1) * g1, g1)
            core[k][pl.ds(row, g1)] = core[k][pl.ds(row, g1)] + part[k][pl.ds(pl.multiple_of(c * half + row, g1), g1)]
            if o:
                copies.append(
                    send(core[k].at[pl.ds(row, g1)], r1[k].at[pl.ds((o - 1) * g1, g1)],
                         s1_s.at[k, o - 1], s1_r.at[k, o - 1], at1(o))
                )
        first.append(copies)

    multiply(0)
    multiply(1)
    begin_first(0)
    multiply(2)
    begin_first(1)
    begin_first(2)

    for copy in mine:
        copy.wait()
    for copy in moved:
        copy.wait_recv()
    for i in range(15):
        first_row = (FRONT + i) * OLD_ROWS
        old[first_row : first_row + OLD_ROWS] = states[i].reshape(OLD_ROWS, LANES)
    slot = slot_ids()
    place = slot + begin
    gathered = [jnp.zeros((WIN, LANES), jnp.float32)] * 3
    for i, (lower, upper) in enumerate(edges):
        inside = (place >= lower) & (place < upper) & (slot < length)
        delta = begin - lower
        row = jnp.clip(delta >> 7, -OUT_ROWS, OLD_ROWS)
        for a in range(3):
            base = (FRONT + 5 * a + i) * OLD_ROWS
            gathered[a] = jnp.where(inside, window(old, base + row, delta & 127), gathered[a])
    for a in range(3):
        kept[a] = gathered[a]

    second = []
    for k, (j0, nj, order) in enumerate(CHUNKS):
        n1, i1, at1, n2, i2, at2 = plan(order)
        g1 = 64 * nj // n1
        g2 = 2 * nj
        for copy in first[k]:
            copy.wait_recv()
        copies = []
        for o in list(range(1, n2)) + [0]:
            row = pl.multiple_of(lax.rem(i2 + o, n2) * g2, g2)
            base = pl.multiple_of(i1 * g1 + row, g2)
            total = core[k][pl.ds(base, g2)]
            for q in range(n1 - 1):
                total = total + r1[k][pl.ds(pl.multiple_of(q * g1 + row, g2), g2)]
            spot = pl.ds(pl.multiple_of(c * 64 * nj + row, g2), g2)
            part[k][spot] = total
            if o:
                copies.append(
                    send(part[k].at[spot], r2[k].at[pl.ds((o - 1) * g2, g2)],
                         s2_s.at[k, o - 1], s2_r.at[k, o - 1], at2(o))
                )
        second.append(copies)

    third = []
    for k, (j0, nj, order) in enumerate(CHUNKS):
        n1, i1, at1, n2, i2, at2 = plan(order)
        g2 = 2 * nj
        for copy in second[k]:
            copy.wait_recv()
        total = part[k][pl.ds(pl.multiple_of(c * 64 * nj + i2 * g2, g2), g2)]
        for q in range(n2 - 1):
            total = total + r2[k][q * g2 : (q + 1) * g2]
        fin[k][2 * g2 : 3 * g2] = total
        third.append([
            send(fin[k].at[pl.ds(2 * g2, g2)], fin[k].at[pl.ds((2 - o) * g2, g2)],
                 rd_s.at[k, i], rd_r.at[k, i], at_d(o))
            for i, o in enumerate(OFFSETS)
        ])

    early = len(sent) - len(OFFSETS) * n
    for copy in sent[:early]:
        copy.wait_send()

    for k, (j0, nj, order) in enumerate(CHUNKS):
        for copy in third[k]:
            copy.wait_recv()
        for m in range(10):
            grad[m * COLS + j0 : m * COLS + j0 + nj] = fin[k][m * nj : (m + 1) * nj]

    live_slot = slot_ids() < length
    delta = begin - (me - 2) * BLOCK
    row = jnp.clip(delta >> 7, 0, GRAD_ROWS - WIN - 1)
    gradient = jnp.where(live_slot, window(grad, row, delta & 127), 0.0)
    master, one, two = kept[0], kept[1], kept[2]
    first_next = BETA_ONE * one + (1.0 - BETA_ONE) * gradient
    second_next = BETA_TWO * two + (1.0 - BETA_TWO) * gradient * gradient
    update = first_next / CORRECT_ONE / (jnp.sqrt(second_next / CORRECT_TWO) + EPSILON)
    master_next = master - LEARN_RATE * (update + DECAY * master)
    for a, value in enumerate((master_next, first_next, second_next)):
        slots[a * WIN : (a + 1) * WIN] = jnp.where(live_slot, value, 0.0)

    for copy in sent[early:]:
        copy.wait_send()


def gather_and_reduce(features, og, live, former, target, keeper, st0, st1, st2):
    n = len(CHUNKS)
    vmem = lambda rows, dtype=jnp.float32: pltpu.VMEM((rows, LANES), dtype)
    scratch = [
        pltpu.VMEM((15, 1, OLD_CAP), jnp.float32),
        vmem(SLOTS * OLD_ROWS),
        pltpu.VMEM((3, WIN, LANES), jnp.float32),
        vmem(GRAD_ROWS),
        pltpu.VMEM((2, ROWS, ROWS), jnp.bfloat16),
        pltpu.VMEM((TOK, COLS * LANES), jnp.bfloat16),
        vmem(TOK, jnp.bfloat16),
        pltpu.VMEM((2, ROWS, TOK), jnp.bfloat16),
    ] + [pltpu.SMEM(v.shape, jnp.int32) for v in (live, keeper, former, target)]
    counts = [(NX, NY) if order == "x" else (NY, NX) for _, _, order in CHUNKS]
    scratch += [vmem(ROWS * nj) for _, nj, _ in CHUNKS]
    scratch += [vmem(64 * nj) for _, nj, _ in CHUNKS]
    scratch += [vmem((n1 - 1) * 64 * nj // n1) for (_, nj, _), (n1, n2) in zip(CHUNKS, counts)]
    scratch += [vmem((n2 - 1) * 2 * nj) for (_, nj, _), (n1, n2) in zip(CHUNKS, counts)]
    scratch += [vmem(10 * nj) for _, nj, _ in CHUNKS]
    dma = lambda *s: pltpu.SemaphoreType.DMA(s)
    scratch += [
        dma(7), dma(7), dma(n), dma(12), dma(12), dma(3), dma(n), dma(n),
        dma(n, 7), dma(n, 7), dma(n, 7), dma(n, 7), dma(n, 4), dma(n, 4), dma(5),
    ]
    vm = pl.BlockSpec(memory_space=pltpu.VMEM)
    return pl.pallas_call(
        main_kernel,
        out_shape=jax.ShapeDtypeStruct((3 * WIN, LANES), jnp.float32),
        in_specs=[pl.BlockSpec(memory_space=pltpu.HBM)] * 9,
        out_specs=vm,
        scratch_shapes=scratch,
        compiler_params=pltpu.CompilerParams(
            collective_id=0, has_side_effects=True, vmem_limit_bytes=56 * 1024 * 1024
        ),
        cost_estimate=pl.CostEstimate(flops=2 * TOK * ROWS * COLS * LANES, bytes_accessed=6_000_000, transcendentals=0),
    )(live, keeper, former, target, features, og, st0, st1, st2)


def lay_out_kernel(slots_in, out_master, out_first, out_second, slots, sem):
    copies = [
        pltpu.make_async_copy(slots_in.at[pl.ds(a * WIN, WIN)], slots.at[a], sem.at[a]) for a in range(3)
    ]
    for copy in copies:
        copy.start()
    for copy, a, out in zip(copies, range(3), (out_master, out_first, out_second)):
        copy.wait()
        value = slots[a]
        for t in range(OUT_ROWS):
            wide = min(LANES, NEW_CAP - t * LANES)
            out[:, t * LANES : t * LANES + wide] = value[t : t + 1, :wide]


def on_device(features, og, live, former, target, keeper, st0, st1, st2):
    slots = gather_and_reduce(features, og, live, former, target, keeper, st0, st1, st2)
    vm = pl.BlockSpec(memory_space=pltpu.VMEM)
    return pl.pallas_call(
        lay_out_kernel,
        out_shape=[jax.ShapeDtypeStruct((1, NEW_CAP), jnp.float32)] * 3,
        in_specs=[pl.BlockSpec(memory_space=pl.ANY)],
        out_specs=[vm] * 3,
        scratch_shapes=[
            pltpu.VMEM((3, WIN, LANES), jnp.float32),
            pltpu.SemaphoreType.DMA((3,)),
        ],
        compiler_params=pltpu.CompilerParams(vmem_limit_bytes=56 * 1024 * 1024),
        cost_estimate=pl.CostEstimate(flops=100_000, bytes_accessed=320_000, transcendentals=0),
    )(slots)


def solution(mesh):
    placed = (
        P(("dp", "tensor"), None),
        P("dp", "tensor"),
        P(),
        P(),
        P(),
        P(),
        P("tensor", "dp"),
        P("tensor", "dp"),
        P("tensor", "dp"),
    )
    return jax.shard_map(
        on_device,
        mesh=mesh,
        in_specs=placed,
        out_specs=(P("tensor", "dp"), P("tensor", "dp"), P("tensor", "dp")),
        check_vma=False,
    )
```

```python
import functools
import jax
import jax.numpy as jnp
from jax import lax
from jax.experimental import pallas as pl
from jax.experimental.pallas import tpu as pltpu
from jax.sharding import PartitionSpec as P

BETA_ONE = 0.9
BETA_TWO = 0.95
EPSILON = 1e-08
DECAY = 0.1
LEARN_RATE = 0.02
CORRECT_ONE = 1.0 - 2.6561398887587544e-05
CORRECT_TWO = 1.0 - 0.005920529220333998

NX, NY, NC = 4, 8, 2
NDP = NX * NY * NC
NZ = 8
ROWS = 128
COLS = 28
TOK = 512
TOK_Z = TOK // NZ
LANES = 128
BLOCK = 7168
OLD_CAP = 12544
OLD_ROWS = OLD_CAP // LANES
NEW_CAP = 12659
OUT_ROWS = 99
WIN = 104
GRAD_ROWS = 304
SLOTS = 20
FRONT = 2
OFFSETS = (-2, -1, 1, 2)

CHUNKS = ((0, 12, "x"), (12, 8, "y"), (20, 8, "x"))


def slot_ids():
    row = lax.broadcasted_iota(jnp.int32, (WIN, LANES), 0)
    return row * LANES + lax.broadcasted_iota(jnp.int32, (WIN, LANES), 1)


def window(ref, row, shift):
    lane = lax.broadcasted_iota(jnp.int32, (WIN, LANES), 1)
    back = lax.rem(LANES - shift, LANES)
    here = pltpu.roll(ref[pl.ds(row, WIN), :], back, 1)
    after = pltpu.roll(ref[pl.ds(row + 1, WIN), :], back, 1)
    return jnp.where(lane < LANES - shift, here, after)


def main_kernel(
    live_in, keeper_in, former_in, target_in, feat, og, st0, st1, st2, slots,
    states, old, kept, grad, pick, og_v, feat_all, mt, live, keeper, former, target, *rest,
):
    n = len(CHUNKS)
    part, core, r1, r2, fin = (rest[k * n : (k + 1) * n] for k in range(5))
    (ag_s, ag_r, og_sem, st_s, st_r, st_loc, co_s, co_r, s1_s, s1_r, s2_s, s2_r, rd_s, rd_r,
     in_sem) = rest[5 * n :]
    me = lax.axis_index("dp")
    z = lax.axis_index("tensor")
    c = lax.rem(me, NC)
    y = lax.rem(me // NC, NY)
    x = me // (NC * NY)

    def dp_of(x_, y_, c_):
        return (x_ * NY + y_) * NC + c_

    def dev(d, z_):
        return {"dp": d, "tensor": z_}

    def at_x(o):
        return dev(dp_of(lax.rem(x + o, NX), y, c), z)

    def at_y(o):
        return dev(dp_of(x, lax.rem(y + o, NY), c), z)

    def at_z(o):
        return dev(me, lax.rem(z + o, NZ))

    def at_d(o):
        return dev(lax.rem(me + o + NDP, NDP), z)

    sibling = dev(dp_of(x, y, 1 - c), z)

    barrier = pltpu.get_barrier_semaphore()
    peers = (
        [at_z(o) for o in range(1, NZ)]
        + [sibling]
        + [at_x(o) for o in range(1, NX)]
        + [at_y(o) for o in range(1, NY)]
        + [at_d(o) for o in OFFSETS]
    )
    for p in peers:
        pl.semaphore_signal(barrier, inc=1, device_id=p, device_id_type=pl.DeviceIdType.MESH)
    my_rows = pl.ds(pl.multiple_of(z * TOK_Z, TOK_Z), TOK_Z)
    small = []
    for i, (a, b) in enumerate(
        ((keeper_in, keeper), (target_in, target), (former_in, former), (live_in, live),
         (feat, feat_all.at[my_rows]))
    ):
        small.append(pltpu.make_async_copy(a, b, in_sem.at[i]))
        small[-1].start()
    local = []
    for k, (j0, nj, _) in enumerate(CHUNKS):
        cols = pl.ds(j0 * LANES, nj * LANES)
        local.append(pltpu.make_async_copy(og.at[:, cols], og_v.at[:, cols], og_sem.at[k]))
        local[-1].start()
    mine = []
    for a, st in enumerate((st0, st1, st2)):
        mine.append(pltpu.make_async_copy(st, states.at[5 * a + 2], st_loc.at[a]))
        mine[-1].start()

    pl.semaphore_wait(barrier, len(peers))

    sent = []

    def send(src, dst, s_sem, r_sem, to):
        copy = pltpu.make_async_remote_copy(
            src_ref=src, dst_ref=dst, send_sem=s_sem, recv_sem=r_sem,
            device_id=to, device_id_type=pl.DeviceIdType.MESH,
        )
        copy.start()
        sent.append(copy)
        return copy

    gather = [
        send(feat, feat_all.at[my_rows], ag_s.at[o - 1], ag_r.at[o - 1], at_z(o))
        for o in (4, 3, 5, 2, 6, 1, 7)
    ]

    moved = []
    for a, st in enumerate((st0, st1, st2)):
        for i, o in enumerate(OFFSETS):
            moved.append(
                send(st, states.at[5 * a + 2 - o], st_s.at[4 * a + i], st_r.at[4 * a + i], at_d(o))
            )

    for copy in small:
        copy.wait()

    def add_up(ref, count, stop):
        return lax.fori_loop(
            0, count, lambda i, t: t + jnp.where(i < stop, ref[i], 0), jnp.int32(0)
        )

    low = jnp.minimum(me, NDP - 2)
    high = jnp.maximum(me - 1, 0)
    at_same = (me < NDP - 1) & (keeper[low] == me)
    at_before = (me > 0) & (keeper[high] == me)
    owner = at_same | at_before
    cursor = jnp.where(at_same, low, high)
    begin = jnp.where(
        at_same, add_up(target, NDP - 1, low), add_up(target, NDP - 1, high)
    )
    length = jnp.where(owner, jnp.where(at_same, target[low], target[high]), 0)
    edges = []
    edge = add_up(former, NDP, me - 2)
    for i in range(5):
        s = me - 2 + i
        inside = (s >= 0) & (s < NDP)
        size = jnp.where(inside, former[jnp.clip(s, 0, NDP - 1)], 0)
        edges.append((edge, edge + size))
        edge = edge + size
    live_count = jnp.where(owner, live[me], 0)

    out_row = lax.broadcasted_iota(jnp.int32, (ROWS, ROWS), 0)
    in_row = lax.broadcasted_iota(jnp.int32, (ROWS, ROWS), 1)
    for w, order in enumerate(("x", "y")):
        cc, b, i = out_row // 64, lax.rem(out_row // 2, 32), lax.rem(out_row, 2)
        if order == "x":
            bx, by = b // NY, lax.rem(b, NY)
        else:
            bx, by = lax.rem(b, NX), b // NX
        pick[w] = (in_row == ((bx * NY + by) * NC + cc) * 2 + i).astype(jnp.float32).astype(jnp.bfloat16)

    for copy in gather:
        copy.wait_recv()

    tok = lax.broadcasted_iota(jnp.int32, (TOK, ROWS), 0)
    masked = jnp.where(tok < live_count, feat_all[...].astype(jnp.float32), 0.0).astype(jnp.bfloat16)
    def reorder(w):
        mt[w] = lax.dot_general(
            pick[w], masked, (((1,), (1,)), ((), ())), preferred_element_type=jnp.float32
        ).astype(jnp.bfloat16)

    reorder(0)
    reorder(1)
    def plan(order):
        if order == "x":
            return NX, x, at_x, NY, y, at_y
        return NY, y, at_y, NX, x, at_x

    cores, first = [], []

    def multiply(k):
        j0, nj, order = CHUNKS[k]
        local[k].wait()
        w = 0 if order == "x" else 1
        for j in range(0, nj, 2):
            out = jnp.dot(
                mt[w],
                og_v[:, (j0 + j) * LANES : (j0 + j + 2) * LANES],
                preferred_element_type=jnp.float32,
            )
            part[k][pl.ds(j, ROWS, stride=nj), :] = out[:, :LANES]
            part[k][pl.ds(j + 1, ROWS, stride=nj), :] = out[:, LANES:]
        half = 64 * nj
        cores.append(
            send(
                part[k].at[pl.ds(pl.multiple_of((1 - c) * half, half), half)],
                core[k], co_s.at[k], co_r.at[k], sibling,
            )
        )

    def begin_first(k):
        j0, nj, order = CHUNKS[k]
        n1, i1, at1, n2, i2, at2 = plan(order)
        g1 = 64 * nj // n1
        half = 64 * nj
        cores[k].wait_recv()
        copies = []
        for o in list(range(1, n1)) + [0]:
            row = pl.multiple_of(lax.rem(i1 + o, n1) * g1, g1)
            core[k][pl.ds(row, g1)] = core[k][pl.ds(row, g1)] + part[k][pl.ds(pl.multiple_of(c * half + row, g1), g1)]
            if o:
                copies.append(
                    send(core[k].at[pl.ds(row, g1)], r1[k].at[pl.ds((o - 1) * g1, g1)],
                         s1_s.at[k, o - 1], s1_r.at[k, o - 1], at1(o))
                )
        first.append(copies)

    multiply(0)
    multiply(1)
    begin_first(0)
    multiply(2)
    begin_first(1)
    begin_first(2)

    for copy in mine:
        copy.wait()
    for copy in moved:
        copy.wait_recv()
    for i in range(15):
        first_row = (FRONT + i) * OLD_ROWS
        old[first_row : first_row + OLD_ROWS] = states[i].reshape(OLD_ROWS, LANES)
    slot = slot_ids()
    place = slot + begin
    gathered = [jnp.zeros((WIN, LANES), jnp.float32)] * 3
    for i, (lower, upper) in enumerate(edges):
        inside = (place >= lower) & (place < upper) & (slot < length)
        delta = begin - lower
        row = jnp.clip(delta >> 7, -OUT_ROWS, OLD_ROWS)
        for a in range(3):
            base = (FRONT + 5 * a + i) * OLD_ROWS
            gathered[a] = jnp.where(inside, window(old, base + row, delta & 127), gathered[a])
    for a in range(3):
        kept[a] = gathered[a]

    second = []
    for k, (j0, nj, order) in enumerate(CHUNKS):
        n1, i1, at1, n2, i2, at2 = plan(order)
        g1 = 64 * nj // n1
        g2 = 2 * nj
        for copy in first[k]:
            copy.wait_recv()
        copies = []
        for o in list(range(1, n2)) + [0]:
            row = pl.multiple_of(lax.rem(i2 + o, n2) * g2, g2)
            base = pl.multiple_of(i1 * g1 + row, g2)
            total = core[k][pl.ds(base, g2)]
            for q in range(n1 - 1):
                total = total + r1[k][pl.ds(pl.multiple_of(q * g1 + row, g2), g2)]
            spot = pl.ds(pl.multiple_of(c * 64 * nj + row, g2), g2)
            part[k][spot] = total
            if o:
                copies.append(
                    send(part[k].at[spot], r2[k].at[pl.ds((o - 1) * g2, g2)],
                         s2_s.at[k, o - 1], s2_r.at[k, o - 1], at2(o))
                )
        second.append(copies)

    third = []
    for k, (j0, nj, order) in enumerate(CHUNKS):
        n1, i1, at1, n2, i2, at2 = plan(order)
        g2 = 2 * nj
        for copy in second[k]:
            copy.wait_recv()
        total = part[k][pl.ds(pl.multiple_of(c * 64 * nj + i2 * g2, g2), g2)]
        for q in range(n2 - 1):
            total = total + r2[k][q * g2 : (q + 1) * g2]
        fin[k][2 * g2 : 3 * g2] = total
        cut, most = nj // 8 * 8, (nj + 7) // 8 * 8
        needed = {2: (cut, g2 - cut), -2: (0, most), 1: (0, g2), -1: (0, g2)}
        third.append([
            send(fin[k].at[pl.ds(2 * g2 + needed[o][0], needed[o][1])],
                 fin[k].at[pl.ds((2 - o) * g2 + needed[o][0], needed[o][1])],
                 rd_s.at[k, i], rd_r.at[k, i], at_d(o))
            for i, o in enumerate(OFFSETS)
        ])

    early = len(sent) - len(OFFSETS) * n
    for copy in sent[:early]:
        copy.wait_send()

    for k, (j0, nj, order) in enumerate(CHUNKS):
        for copy in third[k]:
            copy.wait_recv()
        for m in range(10):
            grad[m * COLS + j0 : m * COLS + j0 + nj] = fin[k][m * nj : (m + 1) * nj]

    live_slot = slot_ids() < length
    delta = begin - (me - 2) * BLOCK
    row = jnp.clip(delta >> 7, 0, GRAD_ROWS - WIN - 1)
    gradient = jnp.where(live_slot, window(grad, row, delta & 127), 0.0)
    master, one, two = kept[0], kept[1], kept[2]
    first_next = BETA_ONE * one + (1.0 - BETA_ONE) * gradient
    second_next = BETA_TWO * two + (1.0 - BETA_TWO) * gradient * gradient
    update = first_next / CORRECT_ONE / (jnp.sqrt(second_next / CORRECT_TWO) + EPSILON)
    master_next = master - LEARN_RATE * (update + DECAY * master)
    for a, value in enumerate((master_next, first_next, second_next)):
        slots[a * WIN : (a + 1) * WIN] = jnp.where(live_slot, value, 0.0)

    for copy in sent[early:]:
        copy.wait_send()


def gather_and_reduce(features, og, live, former, target, keeper, st0, st1, st2):
    n = len(CHUNKS)
    vmem = lambda rows, dtype=jnp.float32: pltpu.VMEM((rows, LANES), dtype)
    scratch = [
        pltpu.VMEM((15, 1, OLD_CAP), jnp.float32),
        vmem(SLOTS * OLD_ROWS),
        pltpu.VMEM((3, WIN, LANES), jnp.float32),
        vmem(GRAD_ROWS),
        pltpu.VMEM((2, ROWS, ROWS), jnp.bfloat16),
        pltpu.VMEM((TOK, COLS * LANES), jnp.bfloat16),
        vmem(TOK, jnp.bfloat16),
        pltpu.VMEM((2, ROWS, TOK), jnp.bfloat16),
    ] + [pltpu.SMEM(v.shape, jnp.int32) for v in (live, keeper, former, target)]
    counts = [(NX, NY) if order == "x" else (NY, NX) for _, _, order in CHUNKS]
    scratch += [vmem(ROWS * nj) for _, nj, _ in CHUNKS]
    scratch += [vmem(64 * nj) for _, nj, _ in CHUNKS]
    scratch += [vmem((n1 - 1) * 64 * nj // n1) for (_, nj, _), (n1, n2) in zip(CHUNKS, counts)]
    scratch += [vmem((n2 - 1) * 2 * nj) for (_, nj, _), (n1, n2) in zip(CHUNKS, counts)]
    scratch += [vmem(10 * nj) for _, nj, _ in CHUNKS]
    dma = lambda *s: pltpu.SemaphoreType.DMA(s)
    scratch += [
        dma(7), dma(7), dma(n), dma(12), dma(12), dma(3), dma(n), dma(n),
        dma(n, 7), dma(n, 7), dma(n, 7), dma(n, 7), dma(n, 4), dma(n, 4), dma(5),
    ]
    vm = pl.BlockSpec(memory_space=pltpu.VMEM)
    return pl.pallas_call(
        main_kernel,
        out_shape=jax.ShapeDtypeStruct((3 * WIN, LANES), jnp.float32),
        in_specs=[pl.BlockSpec(memory_space=pltpu.HBM)] * 9,
        out_specs=vm,
        scratch_shapes=scratch,
        compiler_params=pltpu.CompilerParams(
            collective_id=0, has_side_effects=True, vmem_limit_bytes=56 * 1024 * 1024
        ),
        cost_estimate=pl.CostEstimate(flops=2 * TOK * ROWS * COLS * LANES, bytes_accessed=6_000_000, transcendentals=0),
    )(live, keeper, former, target, features, og, st0, st1, st2)


def lay_out_kernel(slots_in, out_master, out_first, out_second, slots, sem):
    copies = [
        pltpu.make_async_copy(slots_in.at[pl.ds(a * WIN, WIN)], slots.at[a], sem.at[a]) for a in range(3)
    ]
    for copy in copies:
        copy.start()
    for copy, a, out in zip(copies, range(3), (out_master, out_first, out_second)):
        copy.wait()
        value = slots[a]
        for t in range(OUT_ROWS):
            wide = min(LANES, NEW_CAP - t * LANES)
            out[:, t * LANES : t * LANES + wide] = value[t : t + 1, :wide]


def on_device(features, og, live, former, target, keeper, st0, st1, st2):
    slots = gather_and_reduce(features, og, live, former, target, keeper, st0, st1, st2)
    vm = pl.BlockSpec(memory_space=pltpu.VMEM)
    return pl.pallas_call(
        lay_out_kernel,
        out_shape=[jax.ShapeDtypeStruct((1, NEW_CAP), jnp.float32)] * 3,
        in_specs=[pl.BlockSpec(memory_space=pl.ANY)],
        out_specs=[vm] * 3,
        scratch_shapes=[
            pltpu.VMEM((3, WIN, LANES), jnp.float32),
            pltpu.SemaphoreType.DMA((3,)),
        ],
        compiler_params=pltpu.CompilerParams(vmem_limit_bytes=56 * 1024 * 1024),
        cost_estimate=pl.CostEstimate(flops=100_000, bytes_accessed=320_000, transcendentals=0),
    )(slots)


def solution(mesh):
    placed = (
        P(("dp", "tensor"), None),
        P("dp", "tensor"),
        P(),
        P(),
        P(),
        P(),
        P("tensor", "dp"),
        P("tensor", "dp"),
        P("tensor", "dp"),
    )
    return jax.shard_map(
        on_device,
        mesh=mesh,
        in_specs=placed,
        out_specs=(P("tensor", "dp"), P("tensor", "dp"), P("tensor", "dp")),
        check_vma=False,
    )
```
